32 devices in a mesh: exp: 16 (over z, y, core), et: 2 (over x).
Axes of the slice: x: 2, y: 2, z: 4, core: 2. Of those that a mesh axis runs over, the one named last changes fastest.
Arguments:
- tokens: bfloat16 [192, 7168], P(('exp', 'et')), may hold values from -6 to 6
- grad_out: bfloat16 [192, 7168], P(('exp', 'et')), may hold values from -6 to 6
- gates: bfloat16 [192, 8], P(('exp', 'et')), may hold values from 0.049804688 to 1
- expert_ids: int32 [192, 8], P(('exp', 'et')), may hold values from 0 to 15, all different within a row; in each aligned block of 6 rows (0 to 5, 6 to 11, ...) at most 3 rows name the same one
- gate_weight: bfloat16 [16, 7168, 1024], P('exp', None, 'et'), may hold values from -0.0625 to 0.0625
- up_weight: bfloat16 [16, 7168, 1024], P('exp', None, 'et'), may hold values from -0.0625 to 0.0625
- down_weight: bfloat16 [16, 1024, 7168], P('exp', 'et'), may hold values from -0.1875 to 0.1875
Outputs:
- input_grad: bfloat16 [192, 7168], P(('exp', 'et'))
- gate_grad: float32 [192, 8], P(('exp', 'et'))
- gate_weight_grad: bfloat16 [16, 7168, 1024], P('exp', None, 'et')
- up_weight_grad: bfloat16 [16, 7168, 1024], P('exp', None, 'et')
- down_weight_grad: bfloat16 [16, 1024, 7168], P('exp', 'et')
The draws below stay inside these ranges and needn't reach their ends.
Inputs may be any that keep to these rules, and one draw needn't show every extreme that they name: `expert_ids`: each row names 8 different experts. Among the 6 tokens of one device no expert is named by more than 3 tokens, and in every draw some expert is named by exactly 3 tokens of some device.
All inputs are finite; a program needn't handle non-finite values.
Results may differ from the reference program's by a relative error of at most 0.017.
Values may be sent and summed in bfloat16 or wider, within the bound.
No kernel may reach another device: no remote copies, remote signals or barrier semaphores. Data moves between devices by JAX's collectives and lax.ppermute only.
A program may use at most 128 MiB of HBM per device.

```python
import math
import jax
import jax.numpy as jnp
import numpy as np
from jax import lax

D = 7168
TOP = 8
FF = 1024
TOK_DEV = 6
EXPERTS = 16
TOKENS = 192
CAP = 3
N_ET = 2


def level_of(stream_key, extent, pieces, low, top_value):
    loudness, own = 1.0, jax.random.fold_in(stream_key, 6)
    for position, parts in pieces:
        heights = jnp.exp(jax.random.uniform(jax.random.fold_in(own, position), (parts,), jnp.float32, low / len(pieces), top_value / len(pieces)))
        loudness = loudness * jnp.repeat(heights, extent[position] // parts).reshape([-1 if axis == position else 1 for axis in range(len(extent))])
    return loudness


def assign_block(key, own, number, rows, number_of, top, reach, lean):
    sequence = jax.random.permutation(key, number_of)
    packed, common = portions_of(number_of, rows * top, reach, lean, True), portions_of(number_of, rows * top, reach, lean, False)
    places = jnp.arange(number_of)

    def named(lengths, offset_by):
        used = int((lengths > 0).sum())
        fixed = max(1, used // 4)
        moved = fixed + (places - fixed + offset_by * (used - fixed)) % max(1, number_of - fixed)
        return jnp.zeros((number_of,), jnp.int32).at[sequence[jnp.where(places < fixed, places, moved)]].set(jnp.asarray(lengths, jnp.int32))

    lengths = jnp.where(number % 4 == 0, named(packed, number // 4), named(common, number - number // 4 - 1))
    mixed = jax.random.permutation(jax.random.fold_in(own, 3), number_of)
    giver, taker = mixed[0:number_of // 2 * 2:2], mixed[1:number_of // 2 * 2:2]
    slack = jnp.minimum(lengths[giver] - 1, reach - lengths[taker]) // 2
    slack = jnp.where((giver == sequence[0]) | (taker == sequence[0]) | (lengths[taker] == 0), 0, jnp.maximum(slack, 0))
    moved = jax.random.randint(jax.random.fold_in(own, 4), (number_of // 2,), 0, 1 << 20) % (slack + 1)
    lengths = lengths.at[giver].add(-moved).at[taker].add(moved)
    members = jnp.searchsorted(jnp.cumsum(lengths), jnp.arange(rows * top), side="right").astype(jnp.int32)
    listing = members.reshape(top, rows).T
    listing = listing[jax.random.permutation(jax.random.fold_in(own, 1), rows)]
    offset_by = jax.random.randint(jax.random.fold_in(own, 2), (rows, 1), 0, top)
    return jnp.take_along_axis(listing, (jnp.arange(top)[None, :] + offset_by) % top, axis=1)


def portions_of(amount, total, most, lean, full):
    portions = [(1 << 20) // math.isqrt(rank ** lean) + 1 for rank in range(1, amount + 1)]
    largest = most if full else min(most, max(-(-total // amount), total * portions[0] // sum(portions)))
    least = 1 if total - largest >= amount - 1 else 0
    given, rest = [largest] + [least] * (amount - 1), total - largest - least * (amount - 1)
    while rest > 0:
        free = [i for i in range(1, amount) if given[i] < largest] or [i for i in range(1, amount) if given[i] < most]
        whole, budget = sum([portions[i] for i in free]), rest
        for i in free:
            addition = min(most - given[i], max(1, budget * portions[i] // whole), rest)
            given[i] = given[i] + addition
            rest = rest - addition
    return np.array(given)


def centred(own_key, extent, width, most, shards=(), kind=jnp.bfloat16):
    entries = jax.random.normal(own_key, extent, jnp.float32) * width
    if len(shards) > 0:
        entries = level_of(own_key, extent, shards, -0.22, 0.18) * entries
    return jnp.clip(entries, min=-most, max=most).astype(kind)


def setup_inputs(seed: int = 0) -> dict:
    splits = jax.random.split(jax.random.key(seed), 8)
    tokens = centred(splits[0], (TOKENS, D), 1.0, 6.0, ((0, 32),))
    grad_out = centred(splits[1], (TOKENS, D), 1.0, 6.0, ((0, 32),))
    gates = jnp.clip(jnp.exp(math.log(1.0) - 2.9996462 * jax.random.uniform(splits[2], (TOKENS, TOP), jnp.float32) ** level_of(splits[2], (TOKENS, TOP), ((0, 32),), -0.2, 0.2)), 0.049804688, 1.0).astype(jnp.bfloat16)
    expert_ids_keys = jax.random.split(jax.random.fold_in(splits[3], 1), TOKENS // TOK_DEV)
    expert_ids_turns = jax.random.permutation(jax.random.fold_in(splits[3], 3), TOKENS // TOK_DEV)
    expert_ids = jax.vmap(lambda own, number: assign_block(jax.random.fold_in(splits[3], 2), own, number, TOK_DEV, EXPERTS, TOP, CAP, 2))(expert_ids_keys, expert_ids_turns).reshape((TOKENS, TOP))
    gate_weight = centred(splits[4], (EXPERTS, D, FF), D ** -0.5, 0.0625, ((0, 16), (2, 2)))
    up_weight = centred(splits[5], (EXPERTS, D, FF), D ** -0.5, 0.0625, ((0, 16), (2, 2)))
    down_weight = centred(splits[6], (EXPERTS, FF, D), FF ** -0.5, 0.1875, ((0, 16), (1, 2)))
    return {"tokens": tokens, "grad_out": grad_out, "gates": gates, "expert_ids": expert_ids, "gate_weight": gate_weight, "up_weight": up_weight, "down_weight": down_weight}


def expert_terms(rows_x, rows_dy, rows_g, w_gate, w_up, w_down):
    gate_pre = jnp.dot(rows_x, w_gate, preferred_element_type=jnp.float32)
    up_pre = jnp.dot(rows_x, w_up, preferred_element_type=jnp.float32)
    sigma = jax.nn.sigmoid(gate_pre)
    silu_val = gate_pre * sigma
    act = silu_val * up_pre
    back = lax.dot_general(rows_dy, w_down, (((1,), (1,)), ((), ())), preferred_element_type=jnp.float32)
    product = act * back
    scale = rows_g.astype(jnp.float32)[:, None]
    weighted = (scale * act).astype(jnp.bfloat16)
    dact = scale * back
    grad_gate = (dact * up_pre * sigma * (1.0 + gate_pre * (1.0 - sigma))).astype(jnp.bfloat16)
    grad_up = (dact * silu_val).astype(jnp.bfloat16)
    share = w_gate.shape[1] // N_ET
    inward = jnp.zeros((rows_x.shape[0], rows_x.shape[1]), jnp.float32)
    score = jnp.zeros((rows_x.shape[0],), jnp.float32)
    for index in range(N_ET):
        low = index * share
        high = low + share
        piece = lax.dot_general(grad_gate[:, low:high], w_gate[:, low:high], (((1,), (1,)), ((), ())), preferred_element_type=jnp.float32)
        piece = piece + lax.dot_general(grad_up[:, low:high], w_up[:, low:high], (((1,), (1,)), ((), ())), preferred_element_type=jnp.float32)
        inward = inward + lax.optimization_barrier(piece.astype(jnp.bfloat16)).astype(jnp.float32)
        part_score = jnp.sum(product[:, low:high], axis=1)
        score = score + lax.optimization_barrier(part_score.astype(jnp.bfloat16)).astype(jnp.float32)
    d_gate = lax.dot_general(rows_x, grad_gate, (((0,), (0,)), ((), ())), preferred_element_type=jnp.float32)
    d_up = lax.dot_general(rows_x, grad_up, (((0,), (0,)), ((), ())), preferred_element_type=jnp.float32)
    d_down = lax.dot_general(weighted, rows_dy, (((0,), (0,)), ((), ())), preferred_element_type=jnp.float32)
    return d_gate, d_up, d_down, inward, score


def reference(tokens, grad_out, gates, expert_ids, gate_weight, up_weight, down_weight):
    count = tokens.shape[0]
    depth = tokens.shape[1]
    pairs = count * TOP
    flat = expert_ids.reshape(-1).astype(jnp.int32)
    onehot = (flat[:, None] == jnp.arange(EXPERTS, dtype=jnp.int32)[None, :]).astype(jnp.int32)
    rank = jnp.sum((jnp.cumsum(onehot, axis=0) - onehot) * onehot, axis=1)
    limit = (count // TOK_DEV) * CAP
    slots = flat * limit + rank
    table = jnp.full((EXPERTS * limit,), pairs, jnp.int32).at[slots].set(jnp.arange(pairs, dtype=jnp.int32))
    table = table.reshape(EXPERTS, limit)
    x_pad = jnp.concatenate([tokens, jnp.zeros((1, depth), tokens.dtype)], axis=0)
    dy_pad = jnp.concatenate([grad_out, jnp.zeros((1, depth), grad_out.dtype)], axis=0)
    g_pad = jnp.concatenate([gates.reshape(-1), jnp.zeros((1,), gates.dtype)], axis=0)

    def one_expert(carry, inputs):
        grad_acc, score_acc = carry
        w_gate, w_up, w_down, rows = inputs
        owner = (rows // TOP).astype(jnp.int32)
        terms = expert_terms(x_pad[owner], dy_pad[owner], g_pad[rows], w_gate, w_up, w_down)
        grad_acc = grad_acc.at[owner].add(terms[3])
        score_acc = score_acc.at[rows].set(terms[4])
        return (grad_acc, score_acc), (terms[0].astype(jnp.bfloat16), terms[1].astype(jnp.bfloat16), terms[2].astype(jnp.bfloat16))

    init = (jnp.zeros((count + 1, depth), jnp.float32), jnp.zeros((pairs + 1,), jnp.float32))
    (grad_acc, score_acc), (d_gate, d_up, d_down) = lax.scan(one_expert, init, (gate_weight, up_weight, down_weight, table))
    input_grad = grad_acc[:count].astype(jnp.bfloat16)
    gate_grad = score_acc[:pairs].reshape(count, TOP)
    return (input_grad, gate_grad, d_gate, d_up, d_down)
```

```python
import functools

import jax
import jax.numpy as jnp
from jax import lax
from jax.experimental import pallas as pl
from jax.experimental.pallas import tpu as pltpu
from jax.sharding import PartitionSpec as P

LANES = 128
SPLIT = 4
AXES = ("exp", "et")
F32, BF16 = jnp.float32, jnp.bfloat16
MIB = 1 << 20
VMEM = pl.BlockSpec(memory_space=pltpu.VMEM)


def flips(mesh):
    n_exp, n_et = mesh.shape["exp"], mesh.shape["et"]

    def perm(far):
        pairs = []
        for e in range(n_exp):
            for t in range(n_et):
                e2, t2 = far(e, t)
                pairs.append((e * n_et + t, e2 * n_et + t2))
        return pairs

    def flip_y(e, t):
        return e ^ 2, t

    def flip_x(k):
        return lambda e, t: (e, t ^ k)

    def by_core(first, second):
        return perm(lambda e, t: first(e, t) if e % 2 == 0 else second(e, t))

    along = {"z": [perm(lambda e, t, k=k: (e ^ (4 * k), t)) for k in range(1, n_exp // 4)]}
    along["core"] = perm(lambda e, t: (e ^ 1, t))
    along["y"] = perm(flip_y)
    along["x"] = [perm(flip_x(k)) for k in range(1, n_et)]
    along["first"] = by_core(flip_y, flip_x(1))
    along["second"] = by_core(flip_x(1), flip_y)
    return along


def send(block, pairs):
    return lax.ppermute(block, AXES, pairs)


def params(limit=None):
    return pltpu.CompilerParams(vmem_limit_bytes=(limit or 48) * MIB)


def pack_kernel(x_ref, dy_ref, g_ref, id_ref, t_out, d_out):
    count, depth = x_ref.shape
    part = depth // SPLIT
    wide = t_out.shape[1] - part
    t_out[...] = jnp.zeros_like(t_out)
    for j in range(SPLIT):
        t_out[j * count : (j + 1) * count, :part] = x_ref[:, j * part : (j + 1) * part]
        d_out[j * count : (j + 1) * count, :] = dy_ref[:, j * part : (j + 1) * part]
    lane = lax.broadcasted_iota(jnp.int32, (count, wide), 1)
    total = jnp.zeros((count, wide), F32)
    for k in range(g_ref.shape[1]):
        total = total + jnp.where(id_ref[:, k : k + 1] == lane, g_ref[:, k : k + 1].astype(F32), 0.0)
    t_out[:count, part:] = total.astype(BF16)


def pack(tokens, grad_out, gates, expert_ids, wide):
    count, depth = tokens.shape
    part = depth // SPLIT
    return pl.pallas_call(
        pack_kernel,
        out_shape=(
            jax.ShapeDtypeStruct((SPLIT * count, part + wide), BF16),
            jax.ShapeDtypeStruct((SPLIT * count, part), BF16),
        ),
        in_specs=[VMEM] * 4,
        out_specs=(VMEM, VMEM),
        compiler_params=params(8),
        name="pack",
    )(tokens, grad_out, gates, expert_ids)


def unpack_kernel(count, part, *refs):
    out = refs[-1]
    for i, ref in enumerate(refs[:-1]):
        rows = slice(i * count, (i + 1) * count)
        for j in range(SPLIT):
            out[rows, j * part : (j + 1) * part] = ref[j * count : (j + 1) * count, :part]
        if ref.shape[1] > part:
            out[rows, SPLIT * part :] = ref[:count, part:]


def unpack(blocks, count, part):
    extra = blocks[0].shape[1] - part
    return pl.pallas_call(
        functools.partial(unpack_kernel, count, part),
        out_shape=jax.ShapeDtypeStruct((len(blocks) * count, SPLIT * part + extra), BF16),
        in_specs=[VMEM] * len(blocks),
        out_specs=VMEM,
        compiler_params=params(8),
        name="unpack",
    )(*blocks)


def dot(a, b, over):
    return lax.dot_general(a, b, ((over[:1], over[1:]), ((), ())), preferred_element_type=F32)


def in_kernel(n, depth, mine_ref, *refs):
    blocks, (wg, wu, x, act, sp, sq, wt, named, g_acc, u_acc) = refs[:n], refs[n:]
    step, steps = pl.program_id(0), pl.num_programs(0)
    size = wg.shape[0]
    rows = blocks[0].shape[0]
    cols = pl.ds(pl.multiple_of(step * size, LANES), size)
    for i, ref in enumerate(blocks):
        x[i * rows : (i + 1) * rows, cols] = ref[:, cols]

    @pl.when(step == 0)
    def _():
        g_acc[...] = jnp.zeros_like(g_acc)
        u_acc[...] = jnp.zeros_like(u_acc)

    piece = x[:, cols]
    g_acc[...] += dot(piece, wg[...], (1, 0))
    u_acc[...] += dot(piece, wu[...], (1, 0))

    @pl.when(step == steps - 1)
    def _():
        for i, ref in enumerate(blocks):
            span = slice(i * rows, (i + 1) * rows)
            gates = ref[:, depth:].astype(F32)
            at_mine = lax.broadcasted_iota(jnp.int32, gates.shape, 1) == mine_ref[0]
            gates = jnp.where(at_mine, gates, 0.0)
            named[span, :] = (gates != 0.0).astype(F32)
            scale = jnp.sum(gates, axis=1, keepdims=True)
            gate_pre, up_pre = g_acc[span, :], u_acc[span, :]
            sigma = jax.nn.sigmoid(gate_pre)
            silu = gate_pre * sigma
            hidden = silu * up_pre
            act[span, :] = hidden
            wt[span, :] = (scale * hidden).astype(BF16)
            sp[span, :] = scale * (up_pre * sigma * (1.0 + gate_pre * (1.0 - sigma)))
            sq[span, :] = scale * silu


def into_hidden(mine, blocks, w_gate, w_up, depth):
    n, rows = len(blocks), sum(b.shape[0] for b in blocks)
    ff = w_gate.shape[2]
    size = depth // 7 if depth % (7 * LANES) == 0 else depth // SPLIT
    weight = pl.BlockSpec((None, size, ff), lambda i: (0, i, 0))
    wide = jax.ShapeDtypeStruct((rows, ff), F32)
    return pl.pallas_call(
        functools.partial(in_kernel, n, depth),
        grid=(depth // size,),
        out_shape=(
            jax.ShapeDtypeStruct((rows, depth), BF16),
            wide,
            wide,
            wide,
            jax.ShapeDtypeStruct((rows, ff), BF16),
            jax.ShapeDtypeStruct((rows, blocks[0].shape[1] - depth), F32),
        ),
        in_specs=[pl.BlockSpec(memory_space=pltpu.SMEM)] + [VMEM] * n + [weight, weight],
        out_specs=(VMEM,) * 6,
        scratch_shapes=[pltpu.VMEM((rows, ff), F32)] * 2,
        compiler_params=params(),
        name="into_hidden",
    )(mine, *blocks, w_gate, w_up)


def back_kernel(n, *refs):
    blocks, (wd, act, sp, sq, named, dy, gg, gu, score, acc) = refs[:n], refs[n:]
    step, steps = pl.program_id(0), pl.num_programs(0)
    size = wd.shape[1]
    rows = blocks[0].shape[0]
    cols = pl.ds(pl.multiple_of(step * size, LANES), size)
    for i, ref in enumerate(blocks):
        dy[i * rows : (i + 1) * rows, cols] = ref[:, cols]

    @pl.when(step == 0)
    def _():
        acc[...] = jnp.zeros_like(acc)

    acc[...] += dot(dy[:, cols], wd[...], (1, 1))

    @pl.when(step == steps - 1)
    def _():
        back = acc[...]
        gg[...] = (back * sp[...]).astype(BF16)
        gu[...] = (back * sq[...]).astype(BF16)
        score[...] = (named[...] * jnp.sum(act[...] * back, axis=1, keepdims=True)).astype(BF16)


def back_hidden(blocks, w_down, act, sp, sq, named):
    n, rows = len(blocks), act.shape[0]
    ff, depth = w_down.shape[1:]
    size = depth // 7 if depth % (7 * LANES) == 0 else depth // SPLIT
    half = jax.ShapeDtypeStruct((rows, ff), BF16)
    return pl.pallas_call(
        functools.partial(back_kernel, n),
        grid=(depth // size,),
        out_shape=(
            jax.ShapeDtypeStruct((rows, depth), BF16),
            half,
            half,
            jax.ShapeDtypeStruct(named.shape, BF16),
        ),
        in_specs=[VMEM] * n + [pl.BlockSpec((None, ff, size), lambda i: (0, 0, i))] + [VMEM] * 4,
        out_specs=(VMEM,) * 4,
        scratch_shapes=[pltpu.VMEM((rows, ff), F32)],
        compiler_params=params(),
        name="back_hidden",
    )(*blocks, w_down, act, sp, sq, named)


def inward_kernel(gg, gu, wg, wu, out):
    out[...] = (dot(gg[...], wg[...], (1, 1)) + dot(gu[...], wu[...], (1, 1))).astype(BF16)


def inward(gg, gu, w_gate, w_up, start, stop):
    rows, ff = gg.shape
    size = 512
    first = start // size
    weight = pl.BlockSpec((None, size, ff), lambda i: (0, first + i, 0))
    return pl.pallas_call(
        inward_kernel,
        grid=((stop - start) // size,),
        out_shape=jax.ShapeDtypeStruct((rows, stop - start), BF16),
        in_specs=[VMEM, VMEM, weight, weight],
        out_specs=pl.BlockSpec((rows, size), lambda i: (0, i)),
        compiler_params=params(),
        name="inward",
    )(gg, gu, w_gate, w_up)


def outer_kernel(a, b, out):
    out[...] = dot(a[...], b[...], (0, 0)).astype(BF16)


def outer_tall(a, b):
    rows, depth = a.shape
    ff, size = b.shape[1], 1024
    return pl.pallas_call(
        outer_kernel,
        grid=(depth // size,),
        out_shape=jax.ShapeDtypeStruct((1, depth, ff), BF16),
        in_specs=[pl.BlockSpec((rows, size), lambda i: (0, i)), VMEM],
        out_specs=pl.BlockSpec((None, size, ff), lambda i: (0, i, 0)),
        compiler_params=params(),
        name="outer_tall",
    )(a, b)


def outer_wide(a, b):
    rows, depth = b.shape
    ff, size = a.shape[1], 1024
    return pl.pallas_call(
        outer_kernel,
        grid=(depth // size,),
        out_shape=jax.ShapeDtypeStruct((1, ff, depth), BF16),
        in_specs=[VMEM, pl.BlockSpec((rows, size), lambda i: (0, i))],
        out_specs=pl.BlockSpec((None, ff, size), lambda i: (0, 0, i)),
        compiler_params=params(),
        name="outer_wide",
    )(a, b)


def gather_rows(own, along, count, part):
    near = unpack([own] + [send(own, p) for p in along["z"]], count, part)
    first = send(near, along["first"])
    second = send(near, along["second"])
    both = send(first, along["second"])
    held = [near, first, second, both]
    return held + [send(b, along["core"]) for b in held]


def total_of(own, *parts):
    total = own.astype(F32)
    for part in parts:
        total = total + part.astype(F32)
    return total.astype(BF16)


def return_rows(partial, along):
    half = partial.shape[0] // 2
    partial = total_of(partial[:half], send(partial[half:], along["core"]))
    for way in ("second", "first"):
        half = partial.shape[0] // 2
        partial = total_of(partial[:half], send(partial[half:], along[way]))
    size = partial.shape[0] // (len(along["z"]) + 1)
    parts = [send(partial[(i + 1) * size : (i + 2) * size], p) for i, p in enumerate(along["z"])]
    return total_of(partial[:size], *parts)


def on_device(along, tokens, grad_out, gates, expert_ids, gate_weight, up_weight, down_weight):
    count, depth = tokens.shape
    n_exp = lax.axis_size("exp")
    mine = lax.axis_index("exp")
    wide = -(-n_exp // LANES) * LANES
    part = depth // SPLIT
    own_x, own_dy = pack(tokens, grad_out, gates, expert_ids, wide)
    blocks_x = gather_rows(own_x, along, count, part)
    blocks_dy = gather_rows(own_dy, along, count, part)
    x, act, sp, sq, wt, named = into_hidden(
        mine.reshape(1).astype(jnp.int32), blocks_x, gate_weight, up_weight, depth
    )
    dy, gg, gu, score = back_hidden(blocks_dy, down_weight, act, sp, sq, named)
    middle = depth // 2
    low = inward(gg, gu, gate_weight, up_weight, 0, middle)
    high = inward(gg, gu, gate_weight, up_weight, middle, depth)
    got_low = return_rows(low, along)
    got_high = return_rows(jnp.concatenate([high, score], axis=1), along)
    d_gate = outer_tall(x, gg)
    d_up = outer_tall(x, gu)
    d_down = outer_wide(wt, dy)
    input_grad = jnp.concatenate([got_low, got_high[:, : depth - middle]], axis=1)
    lane = jnp.arange(wide, dtype=jnp.int32)
    by_pair = jnp.where(expert_ids[:, :, None] == lane, got_high[:, None, depth - middle :].astype(F32), 0.0)
    return input_grad, jnp.sum(by_pair, axis=2), d_gate, d_up, d_down


def spread(block, stages):
    for stage in stages:
        block = jnp.concatenate([block] + [send(block, p) for p in stage], axis=0)
    return block


def collect(partial, stages):
    for stage in reversed(stages):
        own = partial.shape[0] // (len(stage) + 1)
        parts = [send(partial[(i + 1) * own : (i + 2) * own], p) for i, p in enumerate(stage)]
        partial = total_of(partial[:own], *parts)
    return partial


def on_device_large(along, tokens, grad_out, gates, expert_ids, gate_weight, up_weight, down_weight):
    stages = [along["z"], [along["y"]], along["x"], [along["core"]]]
    depth = tokens.shape[1]
    n_exp = lax.axis_size("exp")
    wide = -(-n_exp // LANES) * LANES
    named = expert_ids[:, :, None] == jnp.arange(wide, dtype=jnp.int32)
    by_expert = jnp.sum(jnp.where(named, gates.astype(F32)[:, :, None], 0.0), axis=1).astype(BF16)
    rows = spread(jnp.concatenate([tokens, by_expert], axis=1), stages)
    rows_dy = spread(grad_out, stages)
    rows_x, rows_g = rows[:, :depth], rows[:, depth:]
    w_gate, w_up, w_down = gate_weight[0], up_weight[0], down_weight[0]
    at_mine = jnp.arange(wide, dtype=jnp.int32)[None, :] == lax.axis_index("exp")
    scale = jnp.sum(jnp.where(at_mine, rows_g.astype(F32), 0.0), axis=1, keepdims=True)
    gate_pre = dot(rows_x, w_gate, (1, 0))
    up_pre = dot(rows_x, w_up, (1, 0))
    back = dot(rows_dy, w_down, (1, 1))
    sigma = jax.nn.sigmoid(gate_pre)
    silu_val = gate_pre * sigma
    act = silu_val * up_pre
    score = jnp.sum(act * back, axis=1, keepdims=True)
    weighted = (scale * act).astype(BF16)
    dact = scale * back
    grad_gate = (dact * up_pre * sigma * (1.0 + gate_pre * (1.0 - sigma))).astype(BF16)
    grad_up = (dact * silu_val).astype(BF16)
    back_in = dot(grad_gate, w_gate, (1, 1)) + dot(grad_up, w_up, (1, 1))
    scores = jnp.where(at_mine & (scale != 0.0), score, 0.0)
    got = collect(jnp.concatenate([back_in.astype(BF16), scores.astype(BF16)], axis=1), stages)
    d_gate = dot(rows_x, grad_gate, (0, 0)).astype(BF16)
    d_up = dot(rows_x, grad_up, (0, 0)).astype(BF16)
    d_down = dot(weighted, rows_dy, (0, 0)).astype(BF16)
    by_pair = jnp.where(named, got[:, None, depth:].astype(F32), 0.0)
    return got[:, :depth], jnp.sum(by_pair, axis=2), d_gate[None], d_up[None], d_down[None]


def solution(mesh):
    along = flips(mesh)
    small = mesh.shape["et"] == 2
    placed = (
        P(("exp", "et"), None),
        P(("exp", "et"), None),
        P(("exp", "et"), None),
        P(("exp", "et"), None),
        P("exp", None, "et"),
        P("exp", None, "et"),
        P("exp", "et", None),
    )
    return jax.shard_map(
        functools.partial(on_device if small else on_device_large, along),
        mesh=mesh,
        in_specs=placed,
        out_specs=(placed[0], placed[0], placed[4], placed[5], placed[6]),
        check_vma=False,
    )
```

```python
import functools

import jax
import jax.numpy as jnp
from jax import lax
from jax.experimental import pallas as pl
from jax.experimental.pallas import tpu as pltpu
from jax.sharding import PartitionSpec as P

LANES = 128
SPLIT = 4
AXES = ("exp", "et")
F32, BF16 = jnp.float32, jnp.bfloat16
MIB = 1 << 20
HIDDEN_LIMIT = 36
INWARD_LIMIT = 52
VMEM = pl.BlockSpec(memory_space=pltpu.VMEM)
HBM = pl.BlockSpec(memory_space=pltpu.HBM)
ANY = pl.BlockSpec(memory_space=pl.ANY)


def flips(mesh):
    n_exp, n_et = mesh.shape["exp"], mesh.shape["et"]

    def perm(far):
        pairs = []
        for e in range(n_exp):
            for t in range(n_et):
                e2, t2 = far(e, t)
                pairs.append((e * n_et + t, e2 * n_et + t2))
        return pairs

    def flip_y(e, t):
        return e ^ 2, t

    def flip_x(k):
        return lambda e, t: (e, t ^ k)

    def by_core(first, second):
        return perm(lambda e, t: first(e, t) if e % 2 == 0 else second(e, t))

    along = {"z": [perm(lambda e, t, k=k: (e ^ (4 * k), t)) for k in range(1, n_exp // 4)]}
    along["core"] = perm(lambda e, t: (e ^ 1, t))
    along["y"] = perm(flip_y)
    along["x"] = [perm(flip_x(k)) for k in range(1, n_et)]
    along["first"] = by_core(flip_y, flip_x(1))
    along["second"] = by_core(flip_x(1), flip_y)
    return along


def send(block, pairs):
    return lax.ppermute(block, AXES, pairs)


def params(limit=None):
    return pltpu.CompilerParams(vmem_limit_bytes=(limit or 48) * MIB)


def cost(flops, bytes_accessed=0):
    return pl.CostEstimate(flops=flops, bytes_accessed=bytes_accessed, transcendentals=0)


def pack_kernel(x_hbm, dy_hbm, g_hbm, id_hbm, out, x, dy, g, ids, sem):
    copies = [pltpu.make_async_copy(*pair, sem.at[i]) for i, pair in enumerate(
        ((x_hbm, x), (dy_hbm, dy), (g_hbm, g), (id_hbm, ids)))]
    for copy in copies:
        copy.start()
    count, depth = x.shape
    part = depth // SPLIT
    wide = out.shape[1] - part
    out[:, part:] = jnp.zeros((out.shape[0], wide), BF16)
    for copy in copies:
        copy.wait()
    for kind, rows in enumerate((x, dy)):
        for j in range(SPLIT):
            top = (kind * SPLIT + j) * count
            out[top : top + count, :part] = rows[:, j * part : (j + 1) * part]
    lane = lax.broadcasted_iota(jnp.int32, (count, wide), 1)
    total = jnp.zeros((count, wide), F32)
    for k in range(g.shape[1]):
        total = total + jnp.where(ids[:, k : k + 1] == lane, g[:, k : k + 1].astype(F32), 0.0)
    out[:count, part:] = total.astype(BF16)


def pack(*args, wide):
    count, depth = args[0].shape
    return pl.pallas_call(
        pack_kernel,
        out_shape=pltpu.VMEM((2 * SPLIT * count, depth // SPLIT + wide), BF16),
        in_specs=[HBM] * 4,
        out_specs=VMEM,
        scratch_shapes=[pltpu.VMEM(v.shape, v.dtype) for v in args] + [pltpu.SemaphoreType.DMA((4,))],
        compiler_params=params(56),
        name="pack",
    )(*args)


def pair_kernel(count, part, a, b, out):
    for d, ref in enumerate((a, b)):
        for kind in range(2):
            for j in range(SPLIT):
                low = (kind * SPLIT + j) * count
                top = (2 * kind + j // 2) * 2 * count + d * count
                out[top : top + count, (j % 2) * part : (j % 2 + 1) * part] = ref[low : low + count, :part]
        out[d * count : (d + 1) * count, 2 * part :] = ref[:count, part:]


def pair(a, b, count, part):
    return pl.pallas_call(
        functools.partial(pair_kernel, count, part),
        out_shape=jax.ShapeDtypeStruct((2 * SPLIT * count, a.shape[1] + part), BF16),
        in_specs=[VMEM] * 2,
        out_specs=VMEM,
        compiler_params=params(4),
        name="pair",
    )(a, b)


def dot(a, b, over):
    return lax.dot_general(a, b, ((over[:1], over[1:]), ((), ())), preferred_element_type=F32)


def blocks_of(refs, height):
    return [(ref, top) for ref in refs for top in range(0, ref.shape[0], height)]


def assemble(out, near, far, height, kind):
    half = out.shape[1] // 2
    rows = height // 4
    for i, ((a, a_top), (b, b_top)) in enumerate(zip(blocks_of(near, height), blocks_of(far, height), strict=True)):
        for j in range(2):
            top = (2 * kind + j) * rows
            low, high = a[a_top + top : a_top + top + rows, :half], b[b_top + top : b_top + top + rows, :half]
            out[2 * i * rows : 2 * (i + 1) * rows, j * half : (j + 1) * half] = jnp.concatenate([low, high], axis=0)


def scales(near, far, height, first, mine):
    rows = height // 4
    ends = zip(blocks_of(near, height), blocks_of(far, height), strict=True)
    gates = [ref[top : top + rows, first:].astype(F32) for pair in ends for ref, top in pair]
    gates = jnp.concatenate(gates, axis=0)
    gates = jnp.where(lax.broadcasted_iota(jnp.int32, gates.shape, 1) == mine, gates, 0.0)
    return jnp.sum(gates, axis=1, keepdims=True), (gates != 0.0).astype(F32)


def hidden_kernel(n, height, size, mine_ref, *refs):
    near, far, refs = refs[:n], refs[n : 2 * n], refs[2 * n :]
    (wg_hbm, wu_hbm, wd_hbm), (x, dy, wt, gg, gu, score, low), refs = refs[:3], refs[3:10], refs[10:]
    wg, wu, wd, gate_acc, up_acc, sem = refs
    depth, ff = wg.shape
    parts = depth // size
    halves = [pl.ds(i * (ff // 2), ff // 2) for i in range(2)]
    steps = [pl.ds(i * size, size) for i in range(parts)]
    downs = [pltpu.make_async_copy(wd_hbm.at[0, h], wd.at[h], sem.at[i]) for i, h in enumerate(halves)]
    gates = [pltpu.make_async_copy(wg_hbm.at[0, c], wg.at[c], sem.at[2 + i]) for i, c in enumerate(steps)]
    ups = [pltpu.make_async_copy(wu_hbm.at[0, c], wu.at[c], sem.at[2 + parts + i]) for i, c in enumerate(steps)]
    for copy in downs:
        copy.start()
    for pair in zip(gates, ups, strict=True):
        for copy in pair:
            copy.start()
    assemble(dy, near, far, height, 1)
    assemble(x, near, far, height, 0)
    back = []
    for copy, h in zip(downs, halves, strict=True):
        copy.wait()
        back.append(dot(dy[...], wd[h, :], (1, 1)))
    back = jnp.concatenate(back, axis=1)
    for i, c in enumerate(steps):
        gates[i].wait()
        ups[i].wait()
        gate, up = dot(x[:, c], wg[c, :], (1, 0)), dot(x[:, c], wu[c, :], (1, 0))
        gate_acc[...] = gate if i == 0 else gate_acc[...] + gate
        up_acc[...] = up if i == 0 else up_acc[...] + up
    gate_pre, up_pre = gate_acc[...], up_acc[...]
    scale, named = scales(near, far, height, depth // 2, mine_ref[0])
    sigma = jax.nn.sigmoid(gate_pre)
    silu = gate_pre * sigma
    act = silu * up_pre
    wt[...] = (scale * act).astype(BF16)
    score[...] = (named * jnp.sum(act * back, axis=1, keepdims=True)).astype(BF16)
    dact = scale * back
    gg[...] = (dact * up_pre * sigma * (1.0 + gate_pre * (1.0 - sigma))).astype(BF16)
    gu[...] = (dact * silu).astype(BF16)
    for first in range(0, low.shape[1], 512):
        c = pl.ds(first, 512)
        low[:, c] = (dot(gg[...], wg[c, :], (1, 1)) + dot(gu[...], wu[c, :], (1, 1))).astype(BF16)


def hidden(mine, near, far, height, w_gate, w_up, w_down, wide):
    n = len(near)
    rows = sum(b.shape[0] for b in far) // 2
    depth, ff = w_gate.shape[1:]
    size = 1024
    full, half = jax.ShapeDtypeStruct((rows, depth), BF16), jax.ShapeDtypeStruct((rows, ff), BF16)
    return pl.pallas_call(
        functools.partial(hidden_kernel, n, height, size),
        out_shape=(
            full,
            full,
            half,
            half,
            half,
            jax.ShapeDtypeStruct((rows, wide), BF16),
            jax.ShapeDtypeStruct((rows, depth // 2), BF16),
        ),
        in_specs=[pl.BlockSpec(memory_space=pltpu.SMEM)] + [VMEM] * (2 * n) + [ANY] * 3,
        out_specs=(VMEM,) * 7,
        scratch_shapes=[
            pltpu.VMEM((depth, ff), BF16),
            pltpu.VMEM((depth, ff), BF16),
            pltpu.VMEM((ff, depth), BF16),
            pltpu.VMEM((rows, ff), F32),
            pltpu.VMEM((rows, ff), F32),
            pltpu.SemaphoreType.DMA((2 + 2 * (depth // size),)),
        ],
        compiler_params=params(HIDDEN_LIMIT),
        cost_estimate=cost(8 * rows * depth * ff, 6 * depth * ff),
        name="hidden",
    )(mine, *near, *far, w_gate, w_up, w_down)


def inward_kernel(start, size, gg, gu, score, wg_hbm, wu_hbm, out, wg, wu, sem):
    parts = [pl.ds(first, size) for first in range(0, wg.shape[0], size)]
    copies = []
    for i, c in enumerate(parts):
        there = pl.ds(start + i * size, size)
        pair = (
            pltpu.make_async_copy(wg_hbm.at[0, there], wg.at[c], sem.at[2 * i]),
            pltpu.make_async_copy(wu_hbm.at[0, there], wu.at[c], sem.at[2 * i + 1]),
        )
        for copy in pair:
            copy.start()
        copies.append(pair)
    out[:, wg.shape[0] :] = score[...]
    for pair, c in zip(copies, parts, strict=True):
        for copy in pair:
            copy.wait()
        out[:, c] = (dot(gg[...], wg[c, :], (1, 1)) + dot(gu[...], wu[c, :], (1, 1))).astype(BF16)


def inward(gg, gu, score, w_gate, w_up, start):
    rows, ff = gg.shape
    width, size = w_gate.shape[1] - start, 512
    return pl.pallas_call(
        functools.partial(inward_kernel, start, size),
        out_shape=jax.ShapeDtypeStruct((rows, width + score.shape[1]), BF16),
        in_specs=[VMEM] * 3 + [ANY] * 2,
        out_specs=VMEM,
        scratch_shapes=[pltpu.VMEM((width, ff), BF16)] * 2 + [pltpu.SemaphoreType.DMA((2 * (width // size),))],
        compiler_params=params(INWARD_LIMIT),
        cost_estimate=cost(4 * rows * width * ff, 4 * width * ff),
        name="inward",
    )(gg, gu, score, w_gate, w_up)


def outer_kernel(tall, size, a, b, after, out, done, sem):
    copies = []
    for i in range((a if tall else b).shape[1] // size):
        part = pl.ds(i * size, size)
        here = (part, slice(None)) if tall else (slice(None), part)
        left, right = (a[:, part], b[...]) if tall else (a[...], b[:, part])
        done[here] = dot(left, right, (0, 0)).astype(BF16)
        copies.append(pltpu.make_async_copy(done.at[here], out.at[(0, *here)], sem.at[i]))
        copies[-1].start()
    for copy in copies:
        copy.wait()


def outer(a, b, after):
    rows = a.shape[0]
    tall = a.shape[1] > b.shape[1]
    size = 1024
    shape = a.shape[1], b.shape[1]
    return pl.pallas_call(
        functools.partial(outer_kernel, tall, size),
        out_shape=jax.ShapeDtypeStruct((1, *shape), BF16),
        in_specs=[VMEM, VMEM, ANY],
        out_specs=ANY,
        scratch_shapes=[pltpu.VMEM(shape, BF16), pltpu.SemaphoreType.DMA((max(shape) // size,))],
        compiler_params=params(20),
        cost_estimate=cost(2 * rows * shape[0] * shape[1], 2 * shape[0] * shape[1]),
        name="outer",
    )(a, b, after)


def around(near, along):
    first = send(near, along["first"])
    held = [near, first, send(near, along["second"]), send(first, along["second"])]
    return held + [send(b, along["core"]) for b in held]


def total_of(own, *parts):
    total = own.astype(F32)
    for part in parts:
        total = total + part.astype(F32)
    return total.astype(BF16)


def fold(partial, pairs):
    half = partial.shape[0] // 2
    return total_of(partial[:half], send(partial[half:], pairs))


def return_rows(partial, along):
    size = partial.shape[0] // (len(along["z"]) + 1)
    parts = [send(partial[(i + 1) * size : (i + 2) * size], p) for i, p in enumerate(along["z"])]
    return total_of(partial[:size], *parts)


def on_device(along, tokens, grad_out, gates, expert_ids, gate_weight, up_weight, down_weight):
    count, depth = tokens.shape
    n_exp = lax.axis_size("exp")
    mine = lax.axis_index("exp")
    wide = -(-n_exp // LANES) * LANES
    part = depth // SPLIT
    own = pack(tokens, grad_out, gates, expert_ids, wide=wide)
    z1, z2, z3 = along["z"]
    near = pair(own, send(own, z1), count, part)
    height = near.shape[0]
    near = around(near, along)
    far = pair(send(own, z2), send(own, z3), count, part)
    far = around(far, along)
    mine = mine.reshape(1).astype(jnp.int32)
    x, dy, wt, gg, gu, score, low = hidden(mine, near, far, height, gate_weight, up_weight, down_weight, wide)
    middle = depth // 2
    high = inward(gg, gu, score, gate_weight, up_weight, middle)
    low = fold(low, along["core"])
    high = fold(high, along["core"])
    d_gate = outer(x, gg, low)
    low = fold(low, along["second"])
    d_up = outer(x, gu, low)
    high = fold(high, along["second"])
    low = fold(low, along["first"])
    d_down = outer(wt, dy, low)
    high = fold(high, along["first"])
    got_low = return_rows(low, along)
    got_high = return_rows(high, along)
    input_grad = jnp.concatenate([got_low, got_high[:, : depth - middle]], axis=1)
    lane = jnp.arange(wide, dtype=jnp.int32)
    by_pair = jnp.where(expert_ids[:, :, None] == lane, got_high[:, None, depth - middle :].astype(F32), 0.0)
    return input_grad, jnp.sum(by_pair, axis=2), d_gate, d_up, d_down


def spread(block, stages):
    for stage in stages:
        block = jnp.concatenate([block] + [send(block, p) for p in stage], axis=0)
    return block


def collect(partial, stages):
    for stage in reversed(stages):
        own = partial.shape[0] // (len(stage) + 1)
        parts = [send(partial[(i + 1) * own : (i + 2) * own], p) for i, p in enumerate(stage)]
        partial = total_of(partial[:own], *parts)
    return partial


def on_device_large(along, tokens, grad_out, gates, expert_ids, gate_weight, up_weight, down_weight):
    stages = [along["z"], [along["y"]], along["x"], [along["core"]]]
    depth = tokens.shape[1]
    n_exp = lax.axis_size("exp")
    wide = -(-n_exp // LANES) * LANES
    named = expert_ids[:, :, None] == jnp.arange(wide, dtype=jnp.int32)
    by_expert = jnp.sum(jnp.where(named, gates.astype(F32)[:, :, None], 0.0), axis=1).astype(BF16)
    rows = spread(jnp.concatenate([tokens, by_expert], axis=1), stages)
    rows_dy = spread(grad_out, stages)
    rows_x, rows_g = rows[:, :depth], rows[:, depth:]
    w_gate, w_up, w_down = gate_weight[0], up_weight[0], down_weight[0]
    at_mine = jnp.arange(wide, dtype=jnp.int32)[None, :] == lax.axis_index("exp")
    scale = jnp.sum(jnp.where(at_mine, rows_g.astype(F32), 0.0), axis=1, keepdims=True)
    gate_pre = dot(rows_x, w_gate, (1, 0))
    up_pre = dot(rows_x, w_up, (1, 0))
    back = dot(rows_dy, w_down, (1, 1))
    sigma = jax.nn.sigmoid(gate_pre)
    silu_val = gate_pre * sigma
    act = silu_val * up_pre
    score = jnp.sum(act * back, axis=1, keepdims=True)
    weighted = (scale * act).astype(BF16)
    dact = scale * back
    grad_gate = (dact * up_pre * sigma * (1.0 + gate_pre * (1.0 - sigma))).astype(BF16)
    grad_up = (dact * silu_val).astype(BF16)
    back_in = dot(grad_gate, w_gate, (1, 1)) + dot(grad_up, w_up, (1, 1))
    scores = jnp.where(at_mine & (scale != 0.0), score, 0.0)
    got = collect(jnp.concatenate([back_in.astype(BF16), scores.astype(BF16)], axis=1), stages)
    d_gate = dot(rows_x, grad_gate, (0, 0)).astype(BF16)
    d_up = dot(rows_x, grad_up, (0, 0)).astype(BF16)
    d_down = dot(weighted, rows_dy, (0, 0)).astype(BF16)
    by_pair = jnp.where(named, got[:, None, depth:].astype(F32), 0.0)
    return got[:, :depth], jnp.sum(by_pair, axis=2), d_gate[None], d_up[None], d_down[None]


def solution(mesh):
    along = flips(mesh)
    small = mesh.shape["et"] == 2
    placed = (
        P(("exp", "et"), None),
        P(("exp", "et"), None),
        P(("exp", "et"), None),
        P(("exp", "et"), None),
        P("exp", None, "et"),
        P("exp", None, "et"),
        P("exp", "et", None),
    )
    return jax.shard_map(
        functools.partial(on_device if small else on_device_large, along),
        mesh=mesh,
        in_specs=placed,
        out_specs=(placed[0], placed[0], placed[4], placed[5], placed[6]),
        check_vma=False,
    )
```

```python
import functools

import jax
import jax.numpy as jnp
from jax import lax
from jax.experimental import pallas as pl
from jax.experimental.pallas import tpu as pltpu
from jax.sharding import PartitionSpec as P

LANES = 128
SPLIT = 4
AXES = ("exp", "et")
F32, BF16 = jnp.float32, jnp.bfloat16
MIB = 1 << 20
HIDDEN_LIMIT = 36
VMEM = pl.BlockSpec(memory_space=pltpu.VMEM)
HBM = pl.BlockSpec(memory_space=pltpu.HBM)
ANY = pl.BlockSpec(memory_space=pl.ANY)


def flips(mesh):
    n_exp, n_et = mesh.shape["exp"], mesh.shape["et"]

    def perm(far):
        pairs = []
        for e in range(n_exp):
            for t in range(n_et):
                e2, t2 = far(e, t)
                pairs.append((e * n_et + t, e2 * n_et + t2))
        return pairs

    def flip_y(e, t):
        return e ^ 2, t

    def flip_x(k):
        return lambda e, t: (e, t ^ k)

    def by_core(first, second):
        return perm(lambda e, t: first(e, t) if e % 2 == 0 else second(e, t))

    along = {"z": [perm(lambda e, t, k=k: (e ^ (4 * k), t)) for k in range(1, n_exp // 4)]}
    along["core"] = perm(lambda e, t: (e ^ 1, t))
    along["y"] = perm(flip_y)
    along["x"] = [perm(flip_x(k)) for k in range(1, n_et)]
    along["first"] = by_core(flip_y, flip_x(1))
    along["second"] = by_core(flip_x(1), flip_y)
    return along


def send(block, pairs):
    return lax.ppermute(block, AXES, pairs)


def params(limit=None):
    return pltpu.CompilerParams(vmem_limit_bytes=(limit or 48) * MIB)


def cost(flops, bytes_accessed=0):
    return pl.CostEstimate(flops=flops, bytes_accessed=bytes_accessed, transcendentals=0)


def pack_kernel(x_hbm, dy_hbm, g_hbm, id_hbm, out, x, dy, g, ids, sem):
    copies = [pltpu.make_async_copy(*pair, sem.at[i]) for i, pair in enumerate(
        ((x_hbm, x), (dy_hbm, dy), (g_hbm, g), (id_hbm, ids)))]
    for copy in copies:
        copy.start()
    count, depth = x.shape
    part = depth // SPLIT
    wide = out.shape[1] - part
    out[:, part:] = jnp.zeros((out.shape[0], wide), BF16)
    for copy in copies:
        copy.wait()
    for kind, rows in enumerate((x, dy)):
        for j in range(SPLIT):
            top = (kind * SPLIT + j) * count
            out[top : top + count, :part] = rows[:, j * part : (j + 1) * part]
    lane = lax.broadcasted_iota(jnp.int32, (count, wide), 1)
    total = jnp.zeros((count, wide), F32)
    for k in range(g.shape[1]):
        total = total + jnp.where(ids[:, k : k + 1] == lane, g[:, k : k + 1].astype(F32), 0.0)
    out[:count, part:] = total.astype(BF16)


def pack(*args, wide):
    count, depth = args[0].shape
    return pl.pallas_call(
        pack_kernel,
        out_shape=pltpu.VMEM((2 * SPLIT * count, depth // SPLIT + wide), BF16),
        in_specs=[HBM] * 4,
        out_specs=VMEM,
        scratch_shapes=[pltpu.VMEM(v.shape, v.dtype) for v in args] + [pltpu.SemaphoreType.DMA((4,))],
        compiler_params=params(56),
        name="pack",
    )(*args)


def pair_kernel(count, part, a, b, out):
    for d, ref in enumerate((a, b)):
        for kind in range(2):
            for j in range(SPLIT):
                low = (kind * SPLIT + j) * count
                top = (2 * kind + j // 2) * 2 * count + d * count
                out[top : top + count, (j % 2) * part : (j % 2 + 1) * part] = ref[low : low + count, :part]
        out[d * count : (d + 1) * count, 2 * part :] = ref[:count, part:]


def pair(a, b, count, part):
    return pl.pallas_call(
        functools.partial(pair_kernel, count, part),
        out_shape=jax.ShapeDtypeStruct((2 * SPLIT * count, a.shape[1] + part), BF16),
        in_specs=[VMEM] * 2,
        out_specs=VMEM,
        compiler_params=params(4),
        name="pair",
    )(a, b)


def dot(a, b, over):
    return lax.dot_general(a, b, ((over[:1], over[1:]), ((), ())), preferred_element_type=F32)


def blocks_of(refs, height):
    return [(ref, top) for ref in refs for top in range(0, ref.shape[0], height)]


def assemble(out, first, refs, height, kind):
    half = out.shape[1] // 2
    rows = height // 4
    blocks = blocks_of(refs, height)
    for i in range(0, len(blocks), 2):
        for j in range(2):
            top = (2 * kind + j) * rows
            both = [ref[at + top : at + top + rows, :half] for ref, at in blocks[i : i + 2]]
            out[first + i * rows : first + (i + 2) * rows, j * half : (j + 1) * half] = jnp.concatenate(both, axis=0)


def scales(refs, height, first, mine):
    gates = [ref[at : at + height // 4, first:].astype(F32) for ref, at in blocks_of(refs, height)]
    gates = jnp.concatenate(gates, axis=0)
    gates = jnp.where(lax.broadcasted_iota(jnp.int32, gates.shape, 1) == mine, gates, 0.0)
    return jnp.sum(gates, axis=1, keepdims=True), (gates != 0.0).astype(F32)


def hidden_kernel(n, height, size, mine_ref, *refs):
    near, far, refs = refs[:n], refs[n : 2 * n], refs[2 * n :]
    (wg_hbm, wu_hbm, wd_hbm), (x, dy, wt, gg, gu, near_in, far_in), refs = refs[:3], refs[3:10], refs[10:]
    wg, wu, wd, gate_acc, up_acc, sem = refs
    depth, ff = wg.shape
    parts = depth // size
    halves = [pl.ds(i * (ff // 2), ff // 2) for i in range(2)]
    steps = [pl.ds(i * size, size) for i in range(parts)]
    downs = [pltpu.make_async_copy(wd_hbm.at[0, h], wd.at[h], sem.at[i]) for i, h in enumerate(halves)]
    gates = [pltpu.make_async_copy(wg_hbm.at[0, c], wg.at[c], sem.at[2 + i]) for i, c in enumerate(steps)]
    ups = [pltpu.make_async_copy(wu_hbm.at[0, c], wu.at[c], sem.at[2 + parts + i]) for i, c in enumerate(steps)]
    for copy in downs:
        copy.start()
    for pair in zip(gates, ups, strict=True):
        for copy in pair:
            copy.start()
    middle = x.shape[0] // 2
    for out, kind in ((dy, 1), (x, 0)):
        assemble(out, 0, near, height, kind)
        assemble(out, middle, far, height, kind)
    back = []
    for copy, h in zip(downs, halves, strict=True):
        copy.wait()
        back.append(dot(dy[...], wd[h, :], (1, 1)))
    back = jnp.concatenate(back, axis=1)
    for i, c in enumerate(steps):
        gates[i].wait()
        ups[i].wait()
        gate, up = dot(x[:, c], wg[c, :], (1, 0)), dot(x[:, c], wu[c, :], (1, 0))
        gate_acc[...] = gate if i == 0 else gate_acc[...] + gate
        up_acc[...] = up if i == 0 else up_acc[...] + up
    gate_pre, up_pre = gate_acc[...], up_acc[...]
    scale, named = scales(near + far, height, depth // 2, mine_ref[0])
    sigma = jax.nn.sigmoid(gate_pre)
    silu = gate_pre * sigma
    act = silu * up_pre
    wt[...] = (scale * act).astype(BF16)
    score = (named * jnp.sum(act * back, axis=1, keepdims=True)).astype(BF16)
    dact = scale * back
    gg[...] = (dact * up_pre * sigma * (1.0 + gate_pre * (1.0 - sigma))).astype(BF16)
    gu[...] = (dact * silu).astype(BF16)
    near_in[:, depth:] = score[:middle]
    far_in[:, depth:] = score[middle:]
    for first in range(0, depth, 512):
        c = pl.ds(first, 512)
        total = (dot(gg[...], wg[c, :], (1, 1)) + dot(gu[...], wu[c, :], (1, 1))).astype(BF16)
        near_in[:, c] = total[:middle]
        far_in[:, c] = total[middle:]


def hidden(mine, near, far, height, w_gate, w_up, w_down, wide):
    n = len(near)
    rows = sum(b.shape[0] for b in far) // 2
    depth, ff = w_gate.shape[1:]
    size = 1024
    full, half = jax.ShapeDtypeStruct((rows, depth), BF16), jax.ShapeDtypeStruct((rows, ff), BF16)
    return pl.pallas_call(
        functools.partial(hidden_kernel, n, height, size),
        out_shape=(
            full,
            full,
            half,
            half,
            half,
            jax.ShapeDtypeStruct((rows // 2, depth + wide), BF16),
            jax.ShapeDtypeStruct((rows // 2, depth + wide), BF16),
        ),
        in_specs=[pl.BlockSpec(memory_space=pltpu.SMEM)] + [VMEM] * (2 * n) + [ANY] * 3,
        out_specs=(VMEM,) * 7,
        scratch_shapes=[
            pltpu.VMEM((depth, ff), BF16),
            pltpu.VMEM((depth, ff), BF16),
            pltpu.VMEM((ff, depth), BF16),
            pltpu.VMEM((rows, ff), F32),
            pltpu.VMEM((rows, ff), F32),
            pltpu.SemaphoreType.DMA((2 + 2 * (depth // size),)),
        ],
        compiler_params=params(HIDDEN_LIMIT),
        cost_estimate=cost(8 * rows * depth * ff, 6 * depth * ff),
        name="hidden",
    )(mine, *near, *far, w_gate, w_up, w_down)


def fold_kernel(own, other, after, out):
    out[...] = (own[: out.shape[0], :].astype(F32) + other[...].astype(F32)).astype(BF16)


def fold_after(partial, pairs, after):
    half = partial.shape[0] // 2
    return pl.pallas_call(
        fold_kernel,
        out_shape=jax.ShapeDtypeStruct((half, partial.shape[1]), BF16),
        in_specs=[VMEM, VMEM, ANY],
        out_specs=VMEM,
        compiler_params=params(6),
        name="fold",
    )(partial, send(partial[half:], pairs), after)


def split_kernel(count, part, own, other, first, second):
    total = (own[: 2 * count, :].astype(F32) + other[...].astype(F32)).astype(BF16)
    for d, out in enumerate((first, second)):
        rows = total[d * count : (d + 1) * count]
        for j in range(SPLIT):
            out[j * count : (j + 1) * count, :part] = rows[:, j * part : (j + 1) * part]
        out[:count, part:] = rows[:, SPLIT * part :]
        out[count:, part:] = jnp.zeros_like(out[count:, part:])


def split(own, other, count, part):
    wide = own.shape[1] - SPLIT * part
    shape = jax.ShapeDtypeStruct((SPLIT * count, part + wide), BF16)
    return pl.pallas_call(
        functools.partial(split_kernel, count, part),
        out_shape=(shape, shape),
        in_specs=[VMEM] * 2,
        out_specs=(VMEM,) * 2,
        compiler_params=params(6),
        name="split",
    )(own, other)


def finish_kernel(part, ids, a, b, c, d, grad, gates):
    count = ids.shape[0]
    total = a[...].astype(F32) + b[...].astype(F32) + c[...].astype(F32) + d[...].astype(F32)
    for j in range(SPLIT):
        grad[:, j * part : (j + 1) * part] = total[j * count : (j + 1) * count, :part].astype(BF16)
    score = total[:count, part:]
    lane = lax.broadcasted_iota(jnp.int32, score.shape, 1)
    for k in range(ids.shape[1]):
        gates[:, k : k + 1] = jnp.sum(jnp.where(lane == ids[:, k : k + 1], score, 0.0), axis=1, keepdims=True)


def finish(ids, parts, part):
    count, top = ids.shape
    return pl.pallas_call(
        functools.partial(finish_kernel, part),
        out_shape=(jax.ShapeDtypeStruct((count, SPLIT * part), BF16), jax.ShapeDtypeStruct((count, top), F32)),
        in_specs=[VMEM] * 5,
        out_specs=(VMEM,) * 2,
        compiler_params=params(6),
        name="finish",
    )(ids, *parts)


def outer_kernel(tall, size, a, b, after, out, ended, done, sem):
    copies = []
    for i in range((a if tall else b).shape[1] // size):
        part = pl.ds(i * size, size)
        here = (part, slice(None)) if tall else (slice(None), part)
        left, right = (a[:, part], b[...]) if tall else (a[...], b[:, part])
        done[here] = dot(left, right, (0, 0)).astype(BF16)
        copies.append(pltpu.make_async_copy(done.at[here], out.at[(0, *here)], sem.at[i]))
        copies[-1].start()
    ended[...] = jnp.zeros_like(ended)
    for copy in copies:
        copy.wait()


def outer(a, b, after):
    rows = a.shape[0]
    tall = a.shape[1] > b.shape[1]
    size = 1024
    shape = a.shape[1], b.shape[1]
    return pl.pallas_call(
        functools.partial(outer_kernel, tall, size),
        out_shape=(jax.ShapeDtypeStruct((1, *shape), BF16), jax.ShapeDtypeStruct((8, LANES), F32)),
        in_specs=[VMEM, VMEM, ANY],
        out_specs=(ANY, VMEM),
        scratch_shapes=[pltpu.VMEM(shape, BF16), pltpu.SemaphoreType.DMA((max(shape) // size,))],
        compiler_params=params(20),
        cost_estimate=cost(2 * rows * shape[0] * shape[1], 2 * shape[0] * shape[1]),
        name="outer",
    )(a, b, after)


def around(near, along):
    first = send(near, along["first"])
    held = [near, first, send(near, along["second"]), send(first, along["second"])]
    return held + [send(b, along["core"]) for b in held]


def total_of(own, *parts):
    total = own.astype(F32)
    for part in parts:
        total = total + part.astype(F32)
    return total.astype(BF16)


def fold(partial, pairs):
    half = partial.shape[0] // 2
    return total_of(partial[:half], send(partial[half:], pairs))


def on_device(along, tokens, grad_out, gates, expert_ids, gate_weight, up_weight, down_weight):
    count, depth = tokens.shape
    n_exp = lax.axis_size("exp")
    mine = lax.axis_index("exp")
    wide = -(-n_exp // LANES) * LANES
    part = depth // SPLIT
    own = pack(tokens, grad_out, gates, expert_ids, wide=wide)
    z1, z2, z3 = along["z"]
    near = pair(own, send(own, z1), count, part)
    height = near.shape[0]
    near = around(near, along)
    far = pair(send(own, z2), send(own, z3), count, part)
    far = around(far, along)
    mine = mine.reshape(1).astype(jnp.int32)
    x, dy, wt, gg, gu, near, far = hidden(mine, near, far, height, gate_weight, up_weight, down_weight, wide)
    far = fold(far, along["core"])
    near = fold(near, along["core"])
    d_gate, ended = outer(x, gg, near)
    far = fold_after(far, along["second"], ended)
    d_up, ended = outer(x, gu, far)
    near = fold_after(near, along["second"], ended)
    far_2, far_3 = split(far, send(far[2 * count :], along["first"]), count, part)
    d_down, _ = outer(wt, dy, far_2)
    own, near_1 = split(near, send(near[2 * count :], along["first"]), count, part)
    parts = [own, send(near_1, z1), send(far_2, z2), send(far_3, z3)]
    input_grad, gate_grad = finish(expert_ids, parts, part)
    return input_grad, gate_grad, d_gate, d_up, d_down


def spread(block, stages):
    for stage in stages:
        block = jnp.concatenate([block] + [send(block, p) for p in stage], axis=0)
    return block


def collect(partial, stages):
    for stage in reversed(stages):
        own = partial.shape[0] // (len(stage) + 1)
        parts = [send(partial[(i + 1) * own : (i + 2) * own], p) for i, p in enumerate(stage)]
        partial = total_of(partial[:own], *parts)
    return partial


def on_device_large(along, tokens, grad_out, gates, expert_ids, gate_weight, up_weight, down_weight):
    stages = [along["z"], [along["y"]], along["x"], [along["core"]]]
    depth = tokens.shape[1]
    n_exp = lax.axis_size("exp")
    wide = -(-n_exp // LANES) * LANES
    named = expert_ids[:, :, None] == jnp.arange(wide, dtype=jnp.int32)
    by_expert = jnp.sum(jnp.where(named, gates.astype(F32)[:, :, None], 0.0), axis=1).astype(BF16)
    rows = spread(jnp.concatenate([tokens, by_expert], axis=1), stages)
    rows_dy = spread(grad_out, stages)
    rows_x, rows_g = rows[:, :depth], rows[:, depth:]
    w_gate, w_up, w_down = gate_weight[0], up_weight[0], down_weight[0]
    at_mine = jnp.arange(wide, dtype=jnp.int32)[None, :] == lax.axis_index("exp")
    scale = jnp.sum(jnp.where(at_mine, rows_g.astype(F32), 0.0), axis=1, keepdims=True)
    gate_pre = dot(rows_x, w_gate, (1, 0))
    up_pre = dot(rows_x, w_up, (1, 0))
    back = dot(rows_dy, w_down, (1, 1))
    sigma = jax.nn.sigmoid(gate_pre)
    silu_val = gate_pre * sigma
    act = silu_val * up_pre
    score = jnp.sum(act * back, axis=1, keepdims=True)
    weighted = (scale * act).astype(BF16)
    dact = scale * back
    grad_gate = (dact * up_pre * sigma * (1.0 + gate_pre * (1.0 - sigma))).astype(BF16)
    grad_up = (dact * silu_val).astype(BF16)
    back_in = dot(grad_gate, w_gate, (1, 1)) + dot(grad_up, w_up, (1, 1))
    scores = jnp.where(at_mine & (scale != 0.0), score, 0.0)
    got = collect(jnp.concatenate([back_in.astype(BF16), scores.astype(BF16)], axis=1), stages)
    d_gate = dot(rows_x, grad_gate, (0, 0)).astype(BF16)
    d_up = dot(rows_x, grad_up, (0, 0)).astype(BF16)
    d_down = dot(weighted, rows_dy, (0, 0)).astype(BF16)
    by_pair = jnp.where(named, got[:, None, depth:].astype(F32), 0.0)
    return got[:, :depth], jnp.sum(by_pair, axis=2), d_gate[None], d_up[None], d_down[None]


def solution(mesh):
    along = flips(mesh)
    small = mesh.shape["et"] == 2
    placed = (
        P(("exp", "et"), None),
        P(("exp", "et"), None),
        P(("exp", "et"), None),
        P(("exp", "et"), None),
        P("exp", None, "et"),
        P("exp", None, "et"),
        P("exp", "et", None),
    )
    return jax.shard_map(
        functools.partial(on_device if small else on_device_large, along),
        mesh=mesh,
        in_specs=placed,
        out_specs=(placed[0], placed[0], placed[4], placed[5], placed[6]),
        check_vma=False,
    )
```

```python
import functools

import jax
import jax.numpy as jnp
from jax import lax
from jax.experimental import pallas as pl
from jax.experimental.pallas import tpu as pltpu
from jax.sharding import PartitionSpec as P

LANES = 128
SPLIT = 4
AXES = ("exp", "et")
F32, BF16 = jnp.float32, jnp.bfloat16
MIB = 1 << 20
HIDDEN_LIMIT = 36
VMEM = pl.BlockSpec(memory_space=pltpu.VMEM)
HBM = pl.BlockSpec(memory_space=pltpu.HBM)
ANY = pl.BlockSpec(memory_space=pl.ANY)


def flips(mesh):
    n_exp, n_et = mesh.shape["exp"], mesh.shape["et"]

    def perm(far):
        pairs = []
        for e in range(n_exp):
            for t in range(n_et):
                e2, t2 = far(e, t)
                pairs.append((e * n_et + t, e2 * n_et + t2))
        return pairs

    def flip_y(e, t):
        return e ^ 2, t

    def flip_x(k):
        return lambda e, t: (e, t ^ k)

    def by_core(first, second):
        return perm(lambda e, t: first(e, t) if e % 2 == 0 else second(e, t))

    along = {"z": [perm(lambda e, t, k=k: (e ^ (4 * k), t)) for k in range(1, n_exp // 4)]}
    along["core"] = perm(lambda e, t: (e ^ 1, t))
    along["y"] = perm(flip_y)
    along["x"] = [perm(flip_x(k)) for k in range(1, n_et)]
    along["first"] = by_core(flip_y, flip_x(1))
    along["second"] = by_core(flip_x(1), flip_y)
    return along


def send(block, pairs):
    return lax.ppermute(block, AXES, pairs)


def params(limit=None):
    return pltpu.CompilerParams(vmem_limit_bytes=(limit or 48) * MIB)


def cost(flops, bytes_accessed=0):
    return pl.CostEstimate(flops=flops, bytes_accessed=bytes_accessed, transcendentals=0)


def pack_kernel(x_hbm, dy_hbm, g_hbm, id_hbm, out, x, dy, g, ids, sem):
    copies = [pltpu.make_async_copy(*pair, sem.at[i]) for i, pair in enumerate(
        ((x_hbm, x), (dy_hbm, dy), (g_hbm, g), (id_hbm, ids)))]
    for copy in copies:
        copy.start()
    count, depth = x.shape
    part = depth // SPLIT
    wide = out.shape[1] - part
    out[:, part:] = jnp.zeros((out.shape[0], wide), BF16)
    for copy in copies:
        copy.wait()
    for kind, rows in enumerate((x, dy)):
        for j in range(SPLIT):
            top = (kind * SPLIT + j) * count
            out[top : top + count, :part] = rows[:, j * part : (j + 1) * part]
    lane = lax.broadcasted_iota(jnp.int32, (count, wide), 1)
    total = jnp.zeros((count, wide), F32)
    for k in range(g.shape[1]):
        total = total + jnp.where(ids[:, k : k + 1] == lane, g[:, k : k + 1].astype(F32), 0.0)
    out[:count, part:] = total.astype(BF16)


def pack(*args, wide):
    count, depth = args[0].shape
    return pl.pallas_call(
        pack_kernel,
        out_shape=pltpu.VMEM((2 * SPLIT * count, depth // SPLIT + wide), BF16),
        in_specs=[HBM] * 4,
        out_specs=VMEM,
        scratch_shapes=[pltpu.VMEM(v.shape, v.dtype) for v in args] + [pltpu.SemaphoreType.DMA((4,))],
        compiler_params=params(56),
        name="pack",
    )(*args)


def pair_kernel(count, part, a, b, out):
    for d, ref in enumerate((a, b)):
        for kind in range(2):
            for j in range(SPLIT):
                low = (kind * SPLIT + j) * count
                top = (2 * kind + j // 2) * 2 * count + d * count
                out[top : top + count, (j % 2) * part : (j % 2 + 1) * part] = ref[low : low + count, :part]
        out[d * count : (d + 1) * count, 2 * part :] = ref[:count, part:]


def pair(a, b, count, part):
    return pl.pallas_call(
        functools.partial(pair_kernel, count, part),
        out_shape=jax.ShapeDtypeStruct((2 * SPLIT * count, a.shape[1] + part), BF16),
        in_specs=[VMEM] * 2,
        out_specs=VMEM,
        compiler_params=params(4),
        name="pair",
    )(a, b)


def dot(a, b, over):
    return lax.dot_general(a, b, ((over[:1], over[1:]), ((), ())), preferred_element_type=F32)


def blocks_of(refs, height):
    return [(ref, top) for ref in refs for top in range(0, ref.shape[0], height)]


def assemble(out, first, refs, height, kind):
    half = out.shape[1] // 2
    rows = height // 4
    blocks = blocks_of(refs, height)
    for i in range(0, len(blocks), 2):
        for j in range(2):
            top = (2 * kind + j) * rows
            both = [ref[at + top : at + top + rows, :half] for ref, at in blocks[i : i + 2]]
            out[first + i * rows : first + (i + 2) * rows, j * half : (j + 1) * half] = jnp.concatenate(both, axis=0)


def scales(refs, height, first, mine):
    gates = [ref[at : at + height // 4, first:].astype(F32) for ref, at in blocks_of(refs, height)]
    gates = jnp.concatenate(gates, axis=0)
    gates = jnp.where(lax.broadcasted_iota(jnp.int32, gates.shape, 1) == mine, gates, 0.0)
    return jnp.sum(gates, axis=1, keepdims=True), (gates != 0.0).astype(F32)


def hidden_kernel(n, height, size, mine_ref, *refs):
    near, far, refs = refs[:n], refs[n : 2 * n], refs[2 * n :]
    (wg_hbm, wu_hbm, wd_hbm), (x, dy, wt, gg, gu, near_in, far_in), refs = refs[:3], refs[3:10], refs[10:]
    wg, wu, wd, gate_acc, up_acc, sem = refs
    depth, ff = wg.shape
    parts = depth // size
    halves = [pl.ds(i * (ff // 2), ff // 2) for i in range(2)]
    steps = [pl.ds(i * size, size) for i in range(parts)]
    downs = [pltpu.make_async_copy(wd_hbm.at[0, h], wd.at[h], sem.at[i]) for i, h in enumerate(halves)]
    gates = [pltpu.make_async_copy(wg_hbm.at[0, c], wg.at[c], sem.at[2 + i]) for i, c in enumerate(steps)]
    ups = [pltpu.make_async_copy(wu_hbm.at[0, c], wu.at[c], sem.at[2 + parts + i]) for i, c in enumerate(steps)]
    for copy in downs:
        copy.start()
    for pair in zip(gates, ups, strict=True):
        for copy in pair:
            copy.start()
    middle = x.shape[0] // 2
    assemble(dy, 0, near, height, 1)
    assemble(dy, middle, far, height, 1)
    for copy in downs:
        copy.wait()
    back = dot(dy[...], wd[...], (1, 1))
    assemble(x, 0, near, height, 0)
    assemble(x, middle, far, height, 0)
    for i, c in enumerate(steps):
        gates[i].wait()
        ups[i].wait()
        gate, up = dot(x[:, c], wg[c, :], (1, 0)), dot(x[:, c], wu[c, :], (1, 0))
        gate_acc[...] = gate if i == 0 else gate_acc[...] + gate
        up_acc[...] = up if i == 0 else up_acc[...] + up
    gate_pre, up_pre = gate_acc[...], up_acc[...]
    scale, named = scales(near + far, height, depth // 2, mine_ref[0])
    sigma = jax.nn.sigmoid(gate_pre)
    silu = gate_pre * sigma
    act = silu * up_pre
    wt[...] = (scale * act).astype(BF16)
    score = (named * jnp.sum(act * back, axis=1, keepdims=True)).astype(BF16)
    dact = scale * back
    gg[...] = (dact * up_pre * sigma * (1.0 + gate_pre * (1.0 - sigma))).astype(BF16)
    gu[...] = (dact * silu).astype(BF16)
    near_in[:, depth:] = score[:middle]
    far_in[:, depth:] = score[middle:]
    for first in range(0, depth, 512):
        c = pl.ds(first, 512)
        total = (dot(gg[...], wg[c, :], (1, 1)) + dot(gu[...], wu[c, :], (1, 1))).astype(BF16)
        near_in[:, c] = total[:middle]
        far_in[:, c] = total[middle:]


def hidden(mine, near, far, height, w_gate, w_up, w_down, wide):
    n = len(near)
    rows = sum(b.shape[0] for b in far) // 2
    depth, ff = w_gate.shape[1:]
    size = 1024
    full, half = jax.ShapeDtypeStruct((rows, depth), BF16), jax.ShapeDtypeStruct((rows, ff), BF16)
    return pl.pallas_call(
        functools.partial(hidden_kernel, n, height, size),
        out_shape=(
            full,
            full,
            half,
            half,
            half,
            jax.ShapeDtypeStruct((rows // 2, depth + wide), BF16),
            jax.ShapeDtypeStruct((rows // 2, depth + wide), BF16),
        ),
        in_specs=[pl.BlockSpec(memory_space=pltpu.SMEM)] + [VMEM] * (2 * n) + [ANY] * 3,
        out_specs=(VMEM,) * 7,
        scratch_shapes=[
            pltpu.VMEM((depth, ff), BF16),
            pltpu.VMEM((depth, ff), BF16),
            pltpu.VMEM((ff, depth), BF16),
            pltpu.VMEM((rows, ff), F32),
            pltpu.VMEM((rows, ff), F32),
            pltpu.SemaphoreType.DMA((2 + 2 * (depth // size),)),
        ],
        compiler_params=params(HIDDEN_LIMIT),
        cost_estimate=cost(8 * rows * depth * ff, 6 * depth * ff),
        name="hidden",
    )(mine, *near, *far, w_gate, w_up, w_down)


def fold_kernel(own, other, after, out):
    out[...] = (own[: out.shape[0], :].astype(F32) + other[...].astype(F32)).astype(BF16)


def fold_after(partial, pairs, after):
    half = partial.shape[0] // 2
    return pl.pallas_call(
        fold_kernel,
        out_shape=jax.ShapeDtypeStruct((half, partial.shape[1]), BF16),
        in_specs=[VMEM, VMEM, ANY],
        out_specs=VMEM,
        compiler_params=params(6),
        name="fold",
    )(partial, send(partial[half:], pairs), after)


def split_kernel(count, part, own, other, first, second):
    total = (own[: 2 * count, :].astype(F32) + other[...].astype(F32)).astype(BF16)
    for d, out in enumerate((first, second)):
        rows = total[d * count : (d + 1) * count]
        for j in range(SPLIT):
            out[j * count : (j + 1) * count, :part] = rows[:, j * part : (j + 1) * part]
        out[:count, part:] = rows[:, SPLIT * part :]
        out[count:, part:] = jnp.zeros_like(out[count:, part:])


def split(own, other, count, part):
    wide = own.shape[1] - SPLIT * part
    shape = jax.ShapeDtypeStruct((SPLIT * count, part + wide), BF16)
    return pl.pallas_call(
        functools.partial(split_kernel, count, part),
        out_shape=(shape, shape),
        in_specs=[VMEM] * 2,
        out_specs=(VMEM,) * 2,
        compiler_params=params(6),
        name="split",
    )(own, other)


def finish_kernel(part, ids, a, b, c, d, grad, gates):
    count = ids.shape[0]
    total = a[...].astype(F32) + b[...].astype(F32) + c[...].astype(F32) + d[...].astype(F32)
    for j in range(SPLIT):
        grad[:, j * part : (j + 1) * part] = total[j * count : (j + 1) * count, :part].astype(BF16)
    score = total[:count, part:]
    lane = lax.broadcasted_iota(jnp.int32, score.shape, 1)
    for k in range(ids.shape[1]):
        gates[:, k : k + 1] = jnp.sum(jnp.where(lane == ids[:, k : k + 1], score, 0.0), axis=1, keepdims=True)


def finish(ids, parts, part):
    count, top = ids.shape
    return pl.pallas_call(
        functools.partial(finish_kernel, part),
        out_shape=(jax.ShapeDtypeStruct((count, SPLIT * part), BF16), jax.ShapeDtypeStruct((count, top), F32)),
        in_specs=[VMEM] * 5,
        out_specs=(VMEM,) * 2,
        compiler_params=params(6),
        name="finish",
    )(ids, *parts)


def outer_kernel(tall, size, a, b, after, out, ended, done, sem):
    copies = []
    whole = (a if tall else b).shape[1]
    edges = [0, size // 4] + list(range(size, whole + 1, size))
    for i, (low, high) in enumerate(zip(edges, edges[1:])):
        part = pl.ds(low, high - low)
        here = (part, slice(None)) if tall else (slice(None), part)
        left, right = (a[:, part], b[...]) if tall else (a[...], b[:, part])
        done[here] = dot(left, right, (0, 0)).astype(BF16)
        copies.append(pltpu.make_async_copy(done.at[here], out.at[(0, *here)], sem.at[i]))
        copies[-1].start()
    ended[...] = jnp.zeros_like(ended)
    for copy in copies:
        copy.wait()


def outer(a, b, after):
    rows = a.shape[0]
    tall = a.shape[1] > b.shape[1]
    size = 1024
    shape = a.shape[1], b.shape[1]
    return pl.pallas_call(
        functools.partial(outer_kernel, tall, size),
        out_shape=(jax.ShapeDtypeStruct((1, *shape), BF16), jax.ShapeDtypeStruct((8, LANES), F32)),
        in_specs=[VMEM, VMEM, ANY],
        out_specs=(ANY, VMEM),
        scratch_shapes=[pltpu.VMEM(shape, BF16), pltpu.SemaphoreType.DMA((max(shape) // size + 1,))],
        compiler_params=params(20),
        cost_estimate=cost(2 * rows * shape[0] * shape[1], 2 * shape[0] * shape[1]),
        name="outer",
    )(a, b, after)


def around(near, along):
    first = send(near, along["first"])
    held = [near, first, send(near, along["second"]), send(first, along["second"])]
    return held + [send(b, along["core"]) for b in held]


def total_of(own, *parts):
    total = own.astype(F32)
    for part in parts:
        total = total + part.astype(F32)
    return total.astype(BF16)


def fold(partial, pairs):
    half = partial.shape[0] // 2
    return total_of(partial[:half], send(partial[half:], pairs))


def on_device(along, tokens, grad_out, gates, expert_ids, gate_weight, up_weight, down_weight):
    count, depth = tokens.shape
    n_exp = lax.axis_size("exp")
    mine = lax.axis_index("exp")
    wide = -(-n_exp // LANES) * LANES
    part = depth // SPLIT
    own = pack(tokens, grad_out, gates, expert_ids, wide=wide)
    z1, z2, z3 = along["z"]
    near = pair(own, send(own, z1), count, part)
    height = near.shape[0]
    near = around(near, along)
    far = pair(send(own, z2), send(own, z3), count, part)
    far = around(far, along)
    mine = mine.reshape(1).astype(jnp.int32)
    x, dy, wt, gg, gu, near, far = hidden(mine, near, far, height, gate_weight, up_weight, down_weight, wide)
    far = fold(far, along["core"])
    near = fold(near, along["core"])
    d_gate, ended = outer(x, gg, near)
    far = fold_after(far, along["second"], ended)
    d_up, ended = outer(x, gu, far)
    near = fold_after(near, along["second"], ended)
    far_2, far_3 = split(far, send(far[2 * count :], along["first"]), count, part)
    d_down, _ = outer(wt, dy, far_2)
    own, near_1 = split(near, send(near[2 * count :], along["first"]), count, part)
    parts = [own, send(near_1, z1), send(far_2, z2), send(far_3, z3)]
    input_grad, gate_grad = finish(expert_ids, parts, part)
    return input_grad, gate_grad, d_gate, d_up, d_down


def spread(block, stages):
    for stage in stages:
        block = jnp.concatenate([block] + [send(block, p) for p in stage], axis=0)
    return block


def collect(partial, stages):
    for stage in reversed(stages):
        own = partial.shape[0] // (len(stage) + 1)
        parts = [send(partial[(i + 1) * own : (i + 2) * own], p) for i, p in enumerate(stage)]
        partial = total_of(partial[:own], *parts)
    return partial


def on_device_large(along, tokens, grad_out, gates, expert_ids, gate_weight, up_weight, down_weight):
    stages = [along["z"], [along["y"]], along["x"], [along["core"]]]
    depth = tokens.shape[1]
    n_exp = lax.axis_size("exp")
    wide = -(-n_exp // LANES) * LANES
    named = expert_ids[:, :, None] == jnp.arange(wide, dtype=jnp.int32)
    by_expert = jnp.sum(jnp.where(named, gates.astype(F32)[:, :, None], 0.0), axis=1).astype(BF16)
    rows = spread(jnp.concatenate([tokens, by_expert], axis=1), stages)
    rows_dy = spread(grad_out, stages)
    rows_x, rows_g = rows[:, :depth], rows[:, depth:]
    w_gate, w_up, w_down = gate_weight[0], up_weight[0], down_weight[0]
    at_mine = jnp.arange(wide, dtype=jnp.int32)[None, :] == lax.axis_index("exp")
    scale = jnp.sum(jnp.where(at_mine, rows_g.astype(F32), 0.0), axis=1, keepdims=True)
    gate_pre = dot(rows_x, w_gate, (1, 0))
    up_pre = dot(rows_x, w_up, (1, 0))
    back = dot(rows_dy, w_down, (1, 1))
    sigma = jax.nn.sigmoid(gate_pre)
    silu_val = gate_pre * sigma
    act = silu_val * up_pre
    score = jnp.sum(act * back, axis=1, keepdims=True)
    weighted = (scale * act).astype(BF16)
    dact = scale * back
    grad_gate = (dact * up_pre * sigma * (1.0 + gate_pre * (1.0 - sigma))).astype(BF16)
    grad_up = (dact * silu_val).astype(BF16)
    back_in = dot(grad_gate, w_gate, (1, 1)) + dot(grad_up, w_up, (1, 1))
    scores = jnp.where(at_mine & (scale != 0.0), score, 0.0)
    got = collect(jnp.concatenate([back_in.astype(BF16), scores.astype(BF16)], axis=1), stages)
    d_gate = dot(rows_x, grad_gate, (0, 0)).astype(BF16)
    d_up = dot(rows_x, grad_up, (0, 0)).astype(BF16)
    d_down = dot(weighted, rows_dy, (0, 0)).astype(BF16)
    by_pair = jnp.where(named, got[:, None, depth:].astype(F32), 0.0)
    return got[:, :depth], jnp.sum(by_pair, axis=2), d_gate[None], d_up[None], d_down[None]


def solution(mesh):
    along = flips(mesh)
    small = mesh.shape["et"] == 2
    placed = (
        P(("exp", "et"), None),
        P(("exp", "et"), None),
        P(("exp", "et"), None),
        P(("exp", "et"), None),
        P("exp", None, "et"),
        P("exp", None, "et"),
        P("exp", "et", None),
    )
    return jax.shard_map(
        functools.partial(on_device if small else on_device_large, along),
        mesh=mesh,
        in_specs=placed,
        out_specs=(placed[0], placed[0], placed[4], placed[5], placed[6]),
        check_vma=False,
    )
```
